32 devices in a mesh: dp: 8 (over y, x, core), fsdp: 4 (over z).
Axes of the slice: x: 2, y: 2, z: 4, core: 2. Of those that a mesh axis runs over, the one named last changes fastest.
Arguments:
- latent: bfloat16 [16, 1024, 1408], P('dp', 'fsdp'), may hold values from -6 to 6
- skip_state: bfloat16 [16, 1024, 1408], P('dp', 'fsdp'), may hold values from -6 to 6
- text_states: bfloat16 [16, 333, 1024], P('dp', None, 'fsdp'), may hold values from -6 to 6
- timestep: int32 [16], P('dp'), may hold values from 0 to 999
- position_grid: int32 [16, 2, 1024], P('dp', None, 'fsdp'), may hold values from 0 to 63, as said below
- cotangent: bfloat16 [16, 1024, 1408], P('dp', 'fsdp'), may hold values from -6 to 6
- skip_gain: float32 [2816], replicated, may hold values from 0.5 to 1.5
- skip_bias: float32 [2816], replicated, may hold values from -1 to 1
- skip_w: bfloat16 [2816, 1408], P('dp', 'fsdp'), may hold values from -0.109375 to 0.109375
- skip_b: float32 [1408], replicated, may hold values from -1 to 1
- ada_w: bfloat16 [1408, 1408], P('dp', 'fsdp'), may hold values from -0.15625 to 0.15625
- ada_b: float32 [1408], replicated, may hold values from -1 to 1
- norm1_gain: float32 [1408], replicated, may hold values from 0.5 to 1.5
- norm1_bias: float32 [1408], replicated, may hold values from -1 to 1
- qkv_w: bfloat16 [1408, 4224], P('dp', 'fsdp'), may hold values from -0.15625 to 0.15625
- qkv_b: float32 [4224], replicated, may hold values from -1 to 1
- qnorm1_gain: float32 [88], replicated, may hold values from 0.5 to 1.5
- qnorm1_bias: float32 [88], replicated, may hold values from -1 to 1
- knorm1_gain: float32 [88], replicated, may hold values from 0.5 to 1.5
- knorm1_bias: float32 [88], replicated, may hold values from -1 to 1
- proj1_w: bfloat16 [1408, 1408], P('dp', 'fsdp'), may hold values from -2.5 to 2.5
- proj1_b: float32 [1408], replicated, may hold values from -1 to 1
- norm3_gain: float32 [1408], replicated, may hold values from 0.5 to 1.5
- norm3_bias: float32 [1408], replicated, may hold values from -1 to 1
- q2_w: bfloat16 [1408, 1408], P('dp', 'fsdp'), may hold values from -0.15625 to 0.15625
- q2_b: float32 [1408], replicated, may hold values from -1 to 1
- kv2_w: bfloat16 [2816, 1024], P('dp', 'fsdp'), may hold values from -0.1875 to 0.1875
- kv2_b: float32 [2816], replicated, may hold values from -1 to 1
- qnorm2_gain: float32 [88], replicated, may hold values from 0.5 to 1.5
- qnorm2_bias: float32 [88], replicated, may hold values from -1 to 1
- knorm2_gain: float32 [88], replicated, may hold values from 0.5 to 1.5
- proj2_w: bfloat16 [1408, 1408], P('dp', 'fsdp'), may hold values from -2 to 2
- proj2_b: float32 [1408], replicated, may hold values from -1 to 1
- norm2_gain: float32 [1408], replicated, may hold values from 0.5 to 1.5
- norm2_bias: float32 [1408], replicated, may hold values from -1 to 1
- fc1_w: bfloat16 [1408, 6144], P('dp', 'fsdp'), may hold values from -0.15625 to 0.15625
- fc1_b: float32 [6144], replicated, may hold values from -1 to 1
- fc2_w: bfloat16 [6144, 1408], P('dp', 'fsdp'), may hold values from -0.078125 to 0.078125
- fc2_b: float32 [1408], replicated, may hold values from -1 to 1
Outputs:
- block_out: bfloat16 [16, 1024, 1408], P('dp', 'fsdp')
- latent_grad: float32 [16, 1024, 1408], P('dp', 'fsdp')
- skip_grad: float32 [16, 1024, 1408], P('dp', 'fsdp')
- text_grad: float32 [16, 333, 1024], P('dp', None, 'fsdp')
- skip_gain_grad: float32 [2816], replicated
- skip_bias_grad: float32 [2816], replicated
- skip_w_grad: float32 [2816, 1408], P('dp', 'fsdp')
- skip_b_grad: float32 [1408], replicated
- ada_w_grad: float32 [1408, 1408], P('dp', 'fsdp')
- ada_b_grad: float32 [1408], replicated
- norm1_gain_grad: float32 [1408], replicated
- norm1_bias_grad: float32 [1408], replicated
- qkv_w_grad: float32 [1408, 4224], P('dp', 'fsdp')
- qkv_b_grad: float32 [4224], replicated
- qnorm1_gain_grad: float32 [88], replicated
- qnorm1_bias_grad: float32 [88], replicated
- knorm1_gain_grad: float32 [88], replicated
- knorm1_bias_grad: float32 [88], replicated
- proj1_w_grad: float32 [1408, 1408], P('dp', 'fsdp')
- proj1_b_grad: float32 [1408], replicated
- norm3_gain_grad: float32 [1408], replicated
- norm3_bias_grad: float32 [1408], replicated
- q2_w_grad: float32 [1408, 1408], P('dp', 'fsdp')
- q2_b_grad: float32 [1408], replicated
- kv2_w_grad: float32 [2816, 1024], P('dp', 'fsdp')
- kv2_b_grad: float32 [2816], replicated
- qnorm2_gain_grad: float32 [88], replicated
- qnorm2_bias_grad: float32 [88], replicated
- knorm2_gain_grad: float32 [88], replicated
- proj2_w_grad: float32 [1408, 1408], P('dp', 'fsdp')
- proj2_b_grad: float32 [1408], replicated
- norm2_gain_grad: float32 [1408], replicated
- norm2_bias_grad: float32 [1408], replicated
- fc1_w_grad: float32 [1408, 6144], P('dp', 'fsdp')
- fc1_b_grad: float32 [6144], replicated
- fc2_w_grad: float32 [6144, 1408], P('dp', 'fsdp')
- fc2_b_grad: float32 [1408], replicated
The draws below stay inside these ranges and needn't reach their ends.
Inputs may be any that keep to these rules, and one draw needn't show every extreme that they name: `position_grid`: in each sequence, token i along the last dimension has row i // W in entry 0 and column i mod W in entry 1, for a power of two W of that sequence that divides 1024; the first sequence has the narrowest grid.
All inputs are finite; a program needn't handle non-finite values.
Results may differ from the reference program's by a relative error of at most 0.028.
Values may be sent and summed in bfloat16 or wider, within the bound.
No kernel may reach another device: no remote copies, remote signals or barrier semaphores. Data moves between devices by JAX's collectives and lax.ppermute only.
A program may use at most 384 MiB of HBM per device.

```python
import math
import jax
import jax.numpy as jnp
from jax import lax

D = 1408
HD = 88
FF = 6144
CTX = 1024
TXT = 333
SEQ_LEN = 1024
SEQ_DEV = 2
SEQS = 16
N_DP = 8


def draw_position_grid(key, part):
    key = jax.random.fold_in(key, 7)
    middle = (SEQ_LEN.bit_length() - 1) // 2
    exponent = jax.random.randint(key, (SEQS,), middle - 1, middle + 2).astype(jnp.int32)
    exponent = exponent.at[0].set(middle - 1)
    widths = jnp.left_shift(jnp.ones((SEQS,), jnp.int32), exponent)
    token_index = jnp.arange(SEQ_LEN, dtype=jnp.int32)
    row_index = token_index[None, :] // widths[:, None]
    col_index = token_index[None, :] % widths[:, None]
    return jnp.stack([row_index, col_index], axis=1).astype(jnp.int32)


def with_ends(values, own_key, smallest, top_value):
    spot = [jax.random.randint(jax.random.fold_in(own_key, axis), (), 0, length) for axis, length in enumerate(values.shape)]
    widest = values.shape.index(max(values.shape))
    neighbour = spot[:widest] + [(spot[widest] + 1) % values.shape[widest]] + spot[widest + 1:]
    return values.at[tuple(spot)].set(smallest).at[tuple(neighbour)].set(top_value)


def raised(values, key, source, target, parts, factor):
    owner, partner = [(jnp.arange(values.shape[position]) // (values.shape[position] // parts)).reshape([-1 if axis == position else 1 for axis in range(values.ndim)]) for position in (source, target)]
    chosen = jax.random.permutation(key, parts)[partner]
    strong = (owner == chosen) | (owner == (partner + parts // 2) % parts)
    return jnp.where(strong, factor * values, values)


def levels(key, shape, cuts, low, top_value):
    loudness, own = 1.0, jax.random.fold_in(key, 6)
    for axis_at, parts in cuts:
        draws = jnp.exp(jax.random.uniform(jax.random.fold_in(own, axis_at), (parts,), jnp.float32, low / len(cuts), top_value / len(cuts)))
        loudness = loudness * jnp.repeat(draws, shape[axis_at] // parts).reshape([-1 if axis == axis_at else 1 for axis in range(len(shape))])
    return loudness


def normal_values(stream_key, shape, scale, most, cuts=(), held_as=jnp.bfloat16):
    gain = levels(stream_key, shape, cuts, -0.22, 0.18) if cuts else 1.0
    values = jax.random.normal(stream_key, shape, jnp.float32) * scale * gain
    return jnp.minimum(jnp.maximum(values, -most), most).astype(held_as)


def bell_draw_with(own_key, dims, deviation, reach, cuts, heavy, kind=jnp.bfloat16):
    values = deviation * jax.random.normal(own_key, dims, jnp.float32)
    if cuts:
        values = values * levels(own_key, dims, cuts, -0.22, 0.18)
    return jnp.clip(raised(values, jax.random.fold_in(own_key, 3), *heavy), -reach, reach).astype(kind)


def setup_inputs(seed: int = 0) -> dict:
    seeds = jax.random.split(jax.random.key(seed), 40)
    return {
        "latent": normal_values(seeds[0], (SEQS, SEQ_LEN, D), 1.0, 6.0, ((0, 8), (1, 4))),
        "skip_state": normal_values(seeds[1], (SEQS, SEQ_LEN, D), 1.0, 6.0, ((0, 8), (1, 4))),
        "text_states": normal_values(seeds[2], (SEQS, TXT, CTX), 1.0, 6.0, ((0, 8), (2, 4))),
        "timestep": with_ends(jax.random.randint(seeds[3], (SEQS,), 0, 1000), jax.random.fold_in(seeds[3], 1), 0, 999).astype(jnp.int32),
        "position_grid": draw_position_grid(jax.random.fold_in(seeds[39], 71), 0),
        "cotangent": bell_draw_with(seeds[5], (SEQS, SEQ_LEN, D), 1.0, 6.0, ((0, 8), (1, 4)), (0, 2, 8, 2.0)),
        "skip_gain": jnp.clip(1.0 + 0.1 * jax.random.normal(seeds[6], (2 * D,), jnp.float32), 0.5, 1.5),
        "skip_bias": normal_values(seeds[7], (2 * D,), 0.2, 1.0, (), jnp.float32),
        "skip_w": normal_values(seeds[8], (2 * D, D), (2 * D) ** -0.5, 0.109375, ((0, 8), (1, 4))),
        "skip_b": normal_values(seeds[9], (D,), 0.2, 1.0, (), jnp.float32),
        "ada_w": normal_values(seeds[10], (D, D), D ** -0.5, 0.15625, ((0, 8), (1, 4))),
        "ada_b": normal_values(seeds[11], (D,), 0.2, 1.0, (), jnp.float32),
        "norm1_gain": jnp.clip(1.0 + 0.1 * jax.random.normal(seeds[12], (D,), jnp.float32), 0.5, 1.5),
        "norm1_bias": normal_values(seeds[13], (D,), 0.2, 1.0, (), jnp.float32),
        "qkv_w": normal_values(seeds[14], (D, 3 * D), D ** -0.5, 0.15625, ((0, 8), (1, 4))),
        "qkv_b": normal_values(seeds[15], (3 * D,), 0.2, 1.0, (), jnp.float32),
        "qnorm1_gain": jnp.clip(1.0 + 0.1 * jax.random.normal(seeds[16], (HD,), jnp.float32), 0.5, 1.5),
        "qnorm1_bias": normal_values(seeds[17], (HD,), 0.2, 1.0, (), jnp.float32),
        "knorm1_gain": jnp.clip(1.0 + 0.1 * jax.random.normal(seeds[18], (HD,), jnp.float32), 0.5, 1.5),
        "knorm1_bias": normal_values(seeds[19], (HD,), 0.2, 1.0, (), jnp.float32),
        "proj1_w": normal_values(seeds[20], (D, D), (max(D // 256, 4)) ** -0.5, 2.5, ((0, 8), (1, 4))),
        "proj1_b": normal_values(seeds[21], (D,), 0.2, 1.0, (), jnp.float32),
        "norm3_gain": jnp.clip(1.0 + 0.1 * jax.random.normal(seeds[22], (D,), jnp.float32), 0.5, 1.5),
        "norm3_bias": normal_values(seeds[23], (D,), 0.2, 1.0, (), jnp.float32),
        "q2_w": normal_values(seeds[24], (D, D), D ** -0.5, 0.15625, ((0, 8), (1, 4))),
        "q2_b": normal_values(seeds[25], (D,), 0.2, 1.0, (), jnp.float32),
        "kv2_w": normal_values(seeds[26], (2 * D, CTX), CTX ** -0.5, 0.1875, ((0, 8), (1, 4))),
        "kv2_b": normal_values(seeds[27], (2 * D,), 0.2, 1.0, (), jnp.float32),
        "qnorm2_gain": jnp.clip(1.0 + 0.1 * jax.random.normal(seeds[28], (HD,), jnp.float32), 0.5, 1.5),
        "qnorm2_bias": normal_values(seeds[29], (HD,), 0.2, 1.0, (), jnp.float32),
        "knorm2_gain": jnp.clip(1.0 + 0.1 * jax.random.normal(seeds[30], (HD,), jnp.float32), 0.5, 1.5),
        "proj2_w": normal_values(seeds[31], (D, D), 8 ** -0.5, 2.0, ((0, 8), (1, 4))),
        "proj2_b": normal_values(seeds[32], (D,), 0.2, 1.0, (), jnp.float32),
        "norm2_gain": jnp.clip(1.0 + 0.1 * jax.random.normal(seeds[33], (D,), jnp.float32), 0.5, 1.5),
        "norm2_bias": normal_values(seeds[34], (D,), 0.2, 1.0, (), jnp.float32),
        "fc1_w": normal_values(seeds[35], (D, FF), D ** -0.5, 0.15625, ((0, 8), (1, 4))),
        "fc1_b": normal_values(seeds[36], (FF,), 0.2, 1.0, (), jnp.float32),
        "fc2_w": normal_values(seeds[37], (FF, D), FF ** -0.5, 0.078125, ((0, 8), (1, 4))),
        "fc2_b": normal_values(seeds[38], (D,), 0.2, 1.0, (), jnp.float32),
    }


@jax.custom_vjp
def low(v):
    return lax.optimization_barrier(v.astype(jnp.bfloat16)).astype(jnp.float32)

@jax.custom_vjp
def low_back(v):
    return v

def low_keep(v):
    return (low(v), None)

def low_pass(kept, grad):
    return (grad,)

def back_keep(v):
    return (v, None)

def back_low(kept, grad):
    return (low(grad),)
low.defvjp(low_keep, low_pass)
low_back.defvjp(back_keep, back_low)
highest = lax.Precision.HIGHEST
norm_eps = 1e-06

def layer_norm(values, norm_gain, norm_bias):
    center = values - lax.optimization_barrier(jnp.mean(values, axis=-1, keepdims=True))
    spread = lax.optimization_barrier(jnp.mean(center * center, axis=-1, keepdims=True))
    return center * lax.rsqrt(spread + norm_eps) * norm_gain + norm_bias

def rotary(position_grid, values):
    quarter = values.shape[-1] // 4
    frequency = jnp.exp(jnp.arange(quarter, dtype=jnp.float32) * (-math.log(10000.0) / quarter))
    row_angle = position_grid[:, 0, :, None].astype(jnp.float32) * frequency
    col_angle = position_grid[:, 1, :, None].astype(jnp.float32) * frequency
    angles = jnp.concatenate([row_angle, row_angle, col_angle, col_angle], axis=-1)[:, :, None, :]
    pieces = jnp.split(values, 4, axis=-1)
    turned = jnp.concatenate([-pieces[1], pieces[0], -pieces[3], pieces[2]], axis=-1)
    return values * jnp.cos(angles) + turned * jnp.sin(angles)

def time_embedding(timestep, model_width):
    halfway = model_width // 2
    frequency = jnp.exp(jnp.arange(halfway, dtype=jnp.float32) * (-math.log(10000.0) / halfway))
    angles = timestep.astype(jnp.float32)[:, None] * frequency
    return jnp.concatenate([jnp.cos(angles), jnp.sin(angles)], axis=-1)

def self_heads(position_grid, qkv_rows, qnorm_gain, qnorm_bias, knorm_gain, knorm_bias):
    head_size = qnorm_gain.shape[0]
    shaped = qkv_rows.reshape(qkv_rows.shape[:2] + (3, -1, head_size))
    queries = rotary(position_grid, layer_norm(shaped[:, :, 0], qnorm_gain, qnorm_bias)) * head_size ** (-0.5)
    key_rows = rotary(position_grid, layer_norm(shaped[:, :, 1], knorm_gain, knorm_bias))
    return (queries, key_rows, shaped[:, :, 2])

def cross_queries(position_grid, projected, qnorm_gain, qnorm_bias):
    head_size = qnorm_gain.shape[0]
    shaped = projected.reshape(projected.shape[:2] + (-1, head_size))
    return rotary(position_grid, layer_norm(shaped, qnorm_gain, qnorm_bias)) * head_size ** (-0.5)

def cross_keys(text_kv, knorm_gain):
    head_size = knorm_gain.shape[0]
    half_width = text_kv.shape[-1] // 2
    key_part = text_kv[..., :half_width].reshape(text_kv.shape[:2] + (-1, head_size))
    value_part = text_kv[..., half_width:].reshape(text_kv.shape[:2] + (-1, head_size))
    return (layer_norm(key_part, knorm_gain, jnp.zeros_like(knorm_gain)), value_part)

def attend(triple):
    queries, key_rows, values = triple
    scores = low_back(jnp.einsum('qhd,khd->hqk', queries, key_rows, precision=highest))
    probabilities = jax.nn.softmax(scores, axis=-1)
    return jnp.einsum('hqk,khd->qhd', low(probabilities), values, precision=highest)

def block(params, latent, skip_state, text_states, embed_act, position_grid):
    skip_gain, skip_bias, skip_w, skip_b, ada_w, ada_b, norm1_gain, norm1_bias, qkv_w, qkv_b, qnorm1_gain, qnorm1_bias, knorm1_gain, knorm1_bias, proj1_w, proj1_b, norm3_gain, norm3_bias, q2_w, q2_b, kv2_w, kv2_b, qnorm2_gain, qnorm2_bias, knorm2_gain, proj2_w, proj2_b, norm2_gain, norm2_bias, fc1_w, fc1_b, fc2_w, fc2_b = params
    seq_count, row_count, model_width = latent.shape
    joined = low(layer_norm(jnp.concatenate([latent, skip_state], axis=-1), skip_gain, skip_bias))
    resid_one = low_back(jnp.matmul(joined, skip_w, precision=highest) + skip_b)
    shift = jnp.matmul(embed_act, ada_w, precision=highest) + ada_b
    normed = low(layer_norm(resid_one, norm1_gain, norm1_bias) + shift[:, None, :])
    qkv_rows = low_back(jnp.matmul(normed, qkv_w, precision=highest) + qkv_b)
    queries, key_rows, value_rows = self_heads(position_grid, qkv_rows, qnorm1_gain, qnorm1_bias, knorm1_gain, knorm1_bias)
    mixed = lax.map(jax.checkpoint(attend), (low(queries), low(key_rows), low(value_rows)))
    mixed = low(low_back(mixed.reshape(seq_count, row_count, model_width)))
    resid_two = resid_one + low_back(jnp.matmul(mixed, proj1_w, precision=highest) + proj1_b)
    cross_in = low(layer_norm(resid_two, norm3_gain, norm3_bias))
    cross_proj = low_back(jnp.matmul(cross_in, q2_w, precision=highest) + q2_b)
    cross_q = low(cross_queries(position_grid, cross_proj, qnorm2_gain, qnorm2_bias))
    text_kv = low_back(jnp.einsum('stc,ec->ste', text_states, kv2_w, precision=highest) + kv2_b)
    cross_k, cross_v = cross_keys(text_kv, knorm2_gain)
    cross_mixed = lax.map(jax.checkpoint(attend), (cross_q, low(cross_k), low(cross_v)))
    cross_mixed = low(low_back(cross_mixed.reshape(seq_count, row_count, model_width)))
    resid_three = resid_two + low_back(jnp.matmul(cross_mixed, proj2_w, precision=highest) + proj2_b)
    ffn_in = low(layer_norm(resid_three, norm2_gain, norm2_bias))
    pre_act = low_back(jnp.matmul(ffn_in, fc1_w, precision=highest) + fc1_b)
    hidden = low(jax.nn.gelu(pre_act, approximate=True))
    return resid_three + low_back(jnp.matmul(hidden, fc2_w, precision=highest) + fc2_b)

def reference(latent, skip_state, text_states, timestep, position_grid, cotangent, skip_gain, skip_bias, skip_w, skip_b, ada_w, ada_b, norm1_gain, norm1_bias, qkv_w, qkv_b, qnorm1_gain, qnorm1_bias, knorm1_gain, knorm1_bias, proj1_w, proj1_b, norm3_gain, norm3_bias, q2_w, q2_b, kv2_w, kv2_b, qnorm2_gain, qnorm2_bias, knorm2_gain, proj2_w, proj2_b, norm2_gain, norm2_bias, fc1_w, fc1_b, fc2_w, fc2_b):
    params = tuple((member.astype(jnp.float32) for member in (skip_gain, skip_bias, skip_w, skip_b, ada_w, ada_b, norm1_gain, norm1_bias, qkv_w, qkv_b, qnorm1_gain, qnorm1_bias, knorm1_gain, knorm1_bias, proj1_w, proj1_b, norm3_gain, norm3_bias, q2_w, q2_b, kv2_w, kv2_b, qnorm2_gain, qnorm2_bias, knorm2_gain, proj2_w, proj2_b, norm2_gain, norm2_bias, fc1_w, fc1_b, fc2_w, fc2_b)))

    def regroup(array):
        return array.reshape((N_DP, SEQ_DEV) + array.shape[1:])

    def one_group(totals, group):
        group_latent, group_skip, group_text, group_time, group_grid, group_cot = group
        embed_act = low(jax.nn.silu(time_embedding(group_time, D)))

        def forward(weights_all, latent_in, skip_in, text_in):
            return block(weights_all, latent_in, skip_in, text_in, embed_act, group_grid)
        result, pullback = jax.vjp(forward, params, group_latent.astype(jnp.float32), group_skip.astype(jnp.float32), group_text.astype(jnp.float32))
        grads_all = pullback(group_cot.astype(jnp.float32))
        totals = jax.tree.map(jnp.add, totals, grads_all[0])
        return (totals, (result.astype(jnp.bfloat16), grads_all[1], grads_all[2], grads_all[3]))
    initial = tuple((jnp.zeros_like(member) for member in params))
    totals, stacked = lax.scan(one_group, initial, (regroup(latent), regroup(skip_state), regroup(text_states), regroup(timestep), regroup(position_grid), regroup(cotangent)))
    block_out = stacked[0].reshape(latent.shape)
    latent_grad = stacked[1].reshape(latent.shape)
    skip_grad = stacked[2].reshape(latent.shape)
    text_grad = stacked[3].reshape(text_states.shape)
    return (block_out, latent_grad, skip_grad, text_grad, totals[0], totals[1], totals[2], totals[3], totals[4], totals[5], totals[6], totals[7], totals[8], totals[9], totals[10], totals[11], totals[12], totals[13], totals[14], totals[15], totals[16], totals[17], totals[18], totals[19], totals[20], totals[21], totals[22], totals[23], totals[24], totals[25], totals[26], totals[27], totals[28], totals[29], totals[30], totals[31], totals[32])
```

```python
from functools import partial
import math

import jax
import jax.numpy as jnp
from jax import lax
from jax.experimental import pallas as pl
from jax.experimental.pallas import tpu as pltpu
from jax.sharding import PartitionSpec as P

norm_eps = 1e-06


def layer_norm(values, norm_gain, norm_bias):
    center = values - jnp.mean(values, axis=-1, keepdims=True)
    spread = jnp.mean(center * center, axis=-1, keepdims=True)
    return center * lax.rsqrt(spread + norm_eps) * norm_gain + norm_bias


def time_embedding(timestep, model_width):
    halfway = model_width // 2
    frequency = jnp.exp(jnp.arange(halfway, dtype=jnp.float32) * (-math.log(10000.0) / halfway))
    angles = timestep.astype(jnp.float32)[:, None] * frequency
    return jnp.concatenate([jnp.cos(angles), jnp.sin(angles)], axis=-1)


def text_heads(text_kv, knorm_gain):
    heads = text_kv.reshape(-1, knorm_gain.shape[0], text_kv.shape[1])
    key_heads, value_heads = jnp.split(heads, 2)
    center = key_heads - jnp.mean(key_heads, axis=1, keepdims=True)
    spread = jnp.mean(center * center, axis=1, keepdims=True)
    key_heads = center * lax.rsqrt(spread + norm_eps) * knorm_gain[None, :, None]
    return jnp.concatenate([key_heads, value_heads])


def gelu_tanh(pre_values):
    return jax.nn.gelu(pre_values, approximate=True)


def project(inputs, weight):
    return jnp.dot(inputs, weight, preferred_element_type=jnp.float32)


def project_back(grad_low, weight):
    return lax.dot_general(
        grad_low,
        weight,
        (((grad_low.ndim - 1,), (1,)), ((), ())),
        preferred_element_type=jnp.float32,
    )


def project_sublanes(inputs_turned, weight):
    return lax.dot_general(
        inputs_turned, weight, (((0,), (0,)), ((), ())), preferred_element_type=jnp.float32
    )


def project_turned(inputs, weight):
    return lax.dot_general(
        weight, inputs, (((0,), (1,)), ((), ())), preferred_element_type=jnp.float32
    )


def project_back_turned(grad_low, weight):
    return lax.dot_general(
        weight, grad_low, (((1,), (1,)), ((), ())), preferred_element_type=jnp.float32
    )


def column_sum(grad_low):
    return jnp.sum(grad_low.reshape(-1, grad_low.shape[-1]), axis=0, dtype=jnp.float32)


def lane_dot(left, right):
    return lax.dot_general(
        left, right, (((1,), (1,)), ((), ())), preferred_element_type=jnp.float32
    )


def row_dot(left, right):
    return lax.dot_general(
        left, right, (((0,), (0,)), ((), ())), preferred_element_type=jnp.float32
    )


def swap_quarters(values):
    quarter = values.shape[0] // 4
    pieces = [values[index * quarter : (index + 1) * quarter] for index in (1, 0, 3, 2)]
    return jnp.concatenate(pieces, axis=0)


def turn_tables(position_grid, head_size):
    quarter = head_size // 4
    frequency = jnp.exp(jnp.arange(quarter, dtype=jnp.float32) * (-math.log(10000.0) / quarter))
    row_angle = frequency[:, None] * position_grid[0].astype(jnp.float32)
    col_angle = frequency[:, None] * position_grid[1].astype(jnp.float32)
    row_sin, col_sin = jnp.sin(row_angle), jnp.sin(col_angle)
    row_cos, col_cos = jnp.cos(row_angle), jnp.cos(col_angle)
    return (
        jnp.concatenate([row_cos, row_cos, col_cos, col_cos]),
        jnp.concatenate([-row_sin, row_sin, -col_sin, col_sin]),
    )


def normalize(values):
    center = values - jnp.mean(values, axis=0, keepdims=True)
    spread = lax.rsqrt(jnp.mean(center * center, axis=0, keepdims=True) + norm_eps)
    return (center * spread, spread)


def turn_kernel(normed_parts, gain_ref, bias_ref, cos_ref, sin_ref, in_ref, out_ref):
    part = pl.program_id(0)

    @pl.when(part < normed_parts)
    def _():
        scaled = normalize(in_ref[0])[0] * gain_ref[0] + bias_ref[0]
        turned = scaled * cos_ref[...] + swap_quarters(scaled) * sin_ref[...]
        factor = jnp.where(part == 0, in_ref.shape[1] ** (-0.5), 1.0)
        out_ref[0] = (turned * factor).astype(out_ref.dtype)

    @pl.when(part >= normed_parts)
    def _():
        out_ref[0] = in_ref[0].astype(out_ref.dtype)


def turn_heads(heads, gains, biases, tables, head_count):
    count, head_size, tokens = heads.shape
    normed_parts = gains.shape[0]
    last = normed_parts - 1
    vector = pl.BlockSpec((1, head_size, 1), lambda part, head: (jnp.minimum(part, last), 0, 0))
    table = pl.BlockSpec((head_size, tokens), lambda part, head: (0, 0))
    block = pl.BlockSpec(
        (1, head_size, tokens), lambda part, head: (part * head_count + head, 0, 0)
    )
    return pl.pallas_call(
        partial(turn_kernel, normed_parts),
        grid=(count // head_count, head_count),
        in_specs=[vector, vector, table, table, block],
        out_specs=block,
        out_shape=jax.ShapeDtypeStruct(heads.shape, jnp.bfloat16),
        compiler_params=pltpu.CompilerParams(vmem_limit_bytes=24 * 2**20),
        cost_estimate=pl.CostEstimate(
            flops=20 * heads.size, bytes_accessed=6 * heads.size, transcendentals=0
        ),
    )(gains[:, :, None], biases[:, :, None], *tables, heads)


def turn_back_kernel(
    normed_parts, gain_ref, cos_ref, sin_ref, in_ref, grad_ref, *refs
):
    part, head = pl.program_id(0), pl.program_id(1)
    out_ref, gain_out, bias_out = refs[-3:]
    gradient = grad_ref[0]
    if len(refs) > 3:
        held = refs[0][0] + refs[1][0].astype(jnp.float32)
        gradient = jnp.where(part == 0, gradient, held)

    @pl.when(part < normed_parts)
    def _():
        factor = jnp.where(part == 0, in_ref.shape[1] ** (-0.5), 1.0)
        scaled = gradient * factor
        back = scaled * cos_ref[...] + swap_quarters(scaled * sin_ref[...])
        hat, spread = normalize(in_ref[0])
        gain_term = back * hat

        @pl.when(head == 0)
        def _():
            gain_out[0] = gain_term
            bias_out[0] = back

        @pl.when(head > 0)
        def _():
            gain_out[0] += gain_term
            bias_out[0] += back

        grad_hat = back * gain_ref[0]
        center = grad_hat - jnp.mean(grad_hat, axis=0, keepdims=True)
        along = jnp.mean(grad_hat * hat, axis=0, keepdims=True)
        out_ref[0] = spread * (center - hat * along)

    @pl.when(part >= normed_parts)
    def _():
        out_ref[0] = gradient


def turn_heads_back(heads, query_grads, kv_grads, gains, tables, head_count):
    count, head_size, tokens = heads.shape
    normed_parts = gains.shape[0]
    last = normed_parts - 1
    shape = (1, head_size, tokens)
    vector = pl.BlockSpec((1, head_size, 1), lambda part, head: (jnp.minimum(part, last), 0, 0))
    table = pl.BlockSpec((head_size, tokens), lambda part, head: (0, 0))
    block = pl.BlockSpec(shape, lambda part, head: (part * head_count + head, 0, 0))
    first = pl.BlockSpec(
        shape, lambda part, head: (jnp.where(part == 0, head, head_count - 1), 0, 0)
    )
    later = pl.BlockSpec(
        shape,
        lambda part, head: (jnp.where(part == 0, 0, (part - 1) * head_count + head), 0, 0),
    )
    total = pl.BlockSpec(shape, lambda part, head: (jnp.minimum(part, last), 0, 0))
    in_specs = [vector, table, table, block, first] + [later] * len(kv_grads)
    operands = [gains[:, :, None], *tables, heads, query_grads, *kv_grads]
    kernel = partial(turn_back_kernel, normed_parts)
    totals = jax.ShapeDtypeStruct((normed_parts, head_size, tokens), jnp.float32)
    out, gain_sum, bias_sum = pl.pallas_call(
        kernel,
        grid=(count // head_count, head_count),
        in_specs=in_specs,
        out_specs=[block, total, total],
        out_shape=[jax.ShapeDtypeStruct(heads.shape, jnp.float32), totals, totals],
        compiler_params=pltpu.CompilerParams(vmem_limit_bytes=24 * 2**20),
        cost_estimate=pl.CostEstimate(
            flops=40 * heads.size, bytes_accessed=12 * heads.size, transcendentals=0
        ),
    )(*operands)
    return (out, jnp.sum(gain_sum, axis=-1), jnp.sum(bias_sum, axis=-1))


def joined_rows(refs):
    if len(refs) == 1:
        return refs[0][0]
    return jnp.concatenate([ref[0] for ref in refs], axis=-1)


def attend_kernel(key_count, piece_count, query_ref, *refs):
    keys = joined_rows(refs[:piece_count])
    values = joined_rows(refs[piece_count : 2 * piece_count])
    out_ref, log_ref = refs[2 * piece_count :]
    weights = jnp.exp(row_dot(keys, query_ref[0]))
    if key_count < keys.shape[1]:
        row = lax.broadcasted_iota(jnp.int32, weights.shape, 0)
        weights = jnp.where(row < key_count, weights, 0.0)
    total = jnp.sum(weights, axis=0, keepdims=True)
    mixed = jnp.dot(values, weights.astype(jnp.bfloat16), preferred_element_type=jnp.float32)
    out_ref[0] = mixed / total
    log_ref[0] = jnp.log(total)


def head_block(array, offset):
    return pl.BlockSpec((1,) + array.shape[1:], lambda head: (head + offset, 0, 0))


def attend_cost(head_count, head_size, tokens, keys, products):
    return pl.CostEstimate(
        flops=2 * products * head_count * head_size * tokens * keys,
        bytes_accessed=8 * head_count * head_size * (tokens + keys),
        transcendentals=head_count * tokens * keys,
    )


def attend(queries, pieces, key_count):
    head_count = pieces[0].shape[0] // 2
    head_size, tokens = queries.shape[1:]
    keys = sum(piece.shape[2] for piece in pieces)
    return pl.pallas_call(
        partial(attend_kernel, key_count, len(pieces)),
        grid=(head_count,),
        in_specs=[head_block(queries, 0)]
        + [head_block(piece, 0) for piece in pieces]
        + [head_block(piece, head_count) for piece in pieces],
        out_specs=[
            pl.BlockSpec((1, head_size, tokens), lambda head: (head, 0, 0)),
            pl.BlockSpec((1, 1, tokens), lambda head: (head, 0, 0)),
        ],
        out_shape=[
            jax.ShapeDtypeStruct((head_count, head_size, tokens), jnp.float32),
            jax.ShapeDtypeStruct((head_count, 1, tokens), jnp.float32),
        ],
        compiler_params=pltpu.CompilerParams(vmem_limit_bytes=32 * 2**20),
        cost_estimate=attend_cost(head_count, head_size, tokens, keys, 2),
    )(queries, *pieces, *pieces)


def attend_back_kernel(key_count, piece_count, query_ref, grad_ref, mixed_ref, log_ref, *refs):
    keys = joined_rows(refs[:piece_count])
    values = joined_rows(refs[piece_count : 2 * piece_count])
    outs = refs[2 * piece_count :]
    queries = query_ref[0]
    gradient = grad_ref[0]
    grad_low = gradient.astype(jnp.bfloat16)
    probs = jnp.exp(row_dot(keys, queries) - log_ref[0])
    if key_count < keys.shape[1]:
        row = lax.broadcasted_iota(jnp.int32, probs.shape, 0)
        probs = jnp.where(row < key_count, probs, 0.0)
    along = jnp.sum(grad_low.astype(jnp.float32) * mixed_ref[0], axis=0, keepdims=True)
    grad_scores = (probs * (row_dot(values, grad_low) - along)).astype(jnp.bfloat16)
    outs[0][0] = jnp.dot(keys, grad_scores, preferred_element_type=jnp.float32)
    grad_keys = lane_dot(queries, grad_scores)
    grad_values = lane_dot(grad_low, probs.astype(jnp.bfloat16))
    start = 0
    for index in range(piece_count):
        stop = start + refs[index].shape[2]
        outs[1 + index][0, 0] = grad_keys[:, start:stop].astype(outs[1 + index].dtype)
        outs[1 + index][1, 0] = grad_values[:, start:stop].astype(outs[1 + index].dtype)
        start = stop


def attend_back(queries, gradient, mixed, log_total, pieces, key_count, kinds):
    head_count = pieces[0].shape[0] // 2
    head_size, tokens = queries.shape[1:]
    keys = sum(piece.shape[2] for piece in pieces)
    return pl.pallas_call(
        partial(attend_back_kernel, key_count, len(pieces)),
        grid=(head_count,),
        in_specs=[head_block(array, 0) for array in (queries, gradient, mixed, log_total)]
        + [head_block(piece, 0) for piece in pieces]
        + [head_block(piece, head_count) for piece in pieces],
        out_specs=[pl.BlockSpec((1, head_size, tokens), lambda head: (head, 0, 0))]
        + [
            pl.BlockSpec((2, 1) + piece.shape[1:], lambda head: (0, head, 0, 0)) for piece in pieces
        ],
        out_shape=[jax.ShapeDtypeStruct((head_count, head_size, tokens), jnp.float32)]
        + [
            jax.ShapeDtypeStruct((2, head_count) + piece.shape[1:], kind)
            for piece, kind in zip(pieces, kinds)
        ],
        compiler_params=pltpu.CompilerParams(vmem_limit_bytes=40 * 2**20),
        cost_estimate=attend_cost(head_count, head_size, tokens, keys, 5),
    )(queries, gradient, mixed, log_total, *pieces, *pieces)


def swap_pairs(size, bit):
    return [(index, index ^ bit) for index in range(size)]


def token_routes(dp_size, fsdp_size, flip):
    route = []
    for position in range(dp_size * fsdp_size):
        row, column = divmod(position, fsdp_size)
        core = row % 2
        target_row = row - core + column // 2
        route.append((position, target_row * fsdp_size + 2 * core + (column + flip) % 2))
    return route


def trade(pair, dp_size, fsdp_size):
    return tuple(
        lax.ppermute(part, ("dp", "fsdp"), token_routes(dp_size, fsdp_size, flip))
        for flip, part in enumerate(pair)
    )


def ordered(is_odd, first, second):
    return (jnp.where(is_odd, second, first), jnp.where(is_odd, first, second))


def trade_in(values, is_odd, sizes):
    return trade(ordered(is_odd, values[0], values[1]), *sizes)


def trade_out(first, second, is_odd, sizes):
    return jnp.stack(ordered(is_odd, *trade((first, second), *sizes)))


def column_gather(shard, place, fsdp_size):
    other = lax.ppermute(shard, "fsdp", swap_pairs(fsdp_size, 2))
    held = jnp.stack(ordered(place // 2 == 1, shard, other))
    other = lax.ppermute(held, "fsdp", swap_pairs(fsdp_size, 1))
    even, odd = ordered(place % 2 == 1, held, other)
    return jnp.concatenate([even[0], odd[0], even[1], odd[1]], axis=-1)


def column_scatter(grad_rows, place, fsdp_size):
    blocks = jnp.split(grad_rows, fsdp_size, axis=-1)
    even = jnp.stack([blocks[0], blocks[2]])
    odd = jnp.stack([blocks[1], blocks[3]])
    own, given = ordered(place % 2 == 1, even, odd)
    taken = lax.ppermute(given, "fsdp", swap_pairs(fsdp_size, 1))
    summed = own.astype(jnp.float32) + taken.astype(jnp.float32)
    own, given = ordered(place // 2 == 1, summed[0], summed[1])
    taken = lax.ppermute(given.astype(jnp.bfloat16), "fsdp", swap_pairs(fsdp_size, 2))
    return own + taken.astype(jnp.float32)


def row_gather(rows):
    return lax.all_gather(rows, "dp", axis=0, tiled=True)


def row_scatter(gradient):
    return lax.psum_scatter(gradient, "dp", scatter_dimension=0, tiled=True)


def butterfly_gather(values, axis_name, size, index):
    step = 1
    while step < size:
        other = lax.ppermute(values, axis_name, swap_pairs(size, step))
        values = jnp.concatenate(ordered((index // step) % 2 == 1, values, other), axis=0)
        step *= 2
    return values


def butterfly_sum(values, axis_name, size):
    step = 1
    while step < size:
        values = values + lax.ppermute(values, axis_name, swap_pairs(size, step))
        step *= 2
    return values


def pack_rows(vectors, width):
    rows = []
    for vector in vectors:
        count = -(-vector.shape[0] // width)
        rows.append(jnp.pad(vector, (0, count * width - vector.shape[0])).reshape(count, width))
    return jnp.concatenate(rows)


def unpack_rows(packed, vectors):
    parts = []
    start = 0
    for vector in vectors:
        count = -(-vector.shape[0] // packed.shape[1])
        parts.append(packed[start : start + count].reshape(-1)[: vector.shape[0]])
        start += count
    return parts


def after(values, *earlier):
    corner = (slice(0, 1),) * values.ndim
    wait = sum(
        part[(slice(0, 1),) * part.ndim].reshape((1,) * values.ndim).astype(jnp.float32)
        for part in earlier
    )
    return values.at[corner].set(values[corner] + (wait * 0).astype(values.dtype))


def low_rows(inputs_turned, grad_low):
    return jnp.dot(inputs_turned, grad_low, preferred_element_type=jnp.float32).astype(jnp.bfloat16)


def low_lanes(inputs, grad_turned):
    return lax.dot_general(
        inputs, grad_turned, (((0,), (1,)), ((), ())), preferred_element_type=jnp.float32
    ).astype(jnp.bfloat16)


def back_sublanes(grad_turned, weight):
    return lax.dot_general(
        grad_turned, weight, (((0,), (1,)), ((), ())), preferred_element_type=jnp.float32
    )


def low_grad(inputs, grad_low):
    return lax.dot_general(
        inputs, grad_low, (((0,), (0,)), ((), ())), preferred_element_type=jnp.float32
    ).astype(jnp.bfloat16)


def body(
    dp_size,
    fsdp_size,
    latent,
    skip_state,
    text_states,
    timestep,
    position_grid,
    cotangent,
    skip_gain,
    skip_bias,
    skip_w,
    skip_b,
    ada_w,
    ada_b,
    norm1_gain,
    norm1_bias,
    qkv_w,
    qkv_b,
    qnorm1_gain,
    qnorm1_bias,
    knorm1_gain,
    knorm1_bias,
    proj1_w,
    proj1_b,
    norm3_gain,
    norm3_bias,
    q2_w,
    q2_b,
    kv2_w,
    kv2_b,
    qnorm2_gain,
    qnorm2_bias,
    knorm2_gain,
    proj2_w,
    proj2_b,
    norm2_gain,
    norm2_bias,
    fc1_w,
    fc1_b,
    fc2_w,
    fc2_b,
):
    model_width = latent.shape[-1]
    head_size = qnorm1_gain.shape[0]
    head_count = model_width // head_size
    sizes = (dp_size, fsdp_size)
    place = lax.axis_index("fsdp")
    row_place = lax.axis_index("dp")
    core = row_place % 2
    is_odd = place % 2 == 1
    columns = partial(column_gather, place=place, fsdp_size=fsdp_size)

    pair = swap_pairs(dp_size, 1)
    w_skip = row_gather(columns(skip_w))
    qkv_rows = columns(qkv_w)
    w_qkv = row_gather(after(qkv_rows, w_skip))
    kv2_rows = columns(kv2_w)
    w_kv2 = row_gather(after(kv2_rows, w_qkv))
    square_rows = columns(jnp.concatenate([proj1_w, q2_w, proj2_w]))
    square_rows = square_rows.reshape(3, -1, model_width)
    both_in = jnp.concatenate([latent, skip_state], axis=-1)
    both_in = after(both_in, kv2_rows, square_rows)
    both_in = jnp.concatenate(trade_in(both_in, is_odd, sizes))
    grid_in = jnp.concatenate(trade_in(position_grid, is_odd, sizes), axis=-1)
    tables = turn_tables(grid_in, head_size)

    times = butterfly_gather(timestep, "dp", dp_size, row_place)
    embed_act = jax.nn.silu(time_embedding(times, model_width)).astype(jnp.bfloat16)
    ada_rows = ada_w.shape[0]
    embed_own = lax.dynamic_slice_in_dim(embed_act, row_place * ada_rows, ada_rows, 1)
    shift_part = butterfly_sum(project(embed_own, ada_w), "dp", dp_size)
    own_rows = lax.dynamic_slice_in_dim(shift_part, (row_place // 2) * 4, 4, 0)
    shift_rows = columns(own_rows) + ada_b
    shift = lax.dynamic_slice_in_dim(shift_rows, place, 1, 0)

    joined_in = both_in.astype(jnp.float32)
    joined = layer_norm(joined_in, skip_gain, skip_bias).astype(jnp.bfloat16)
    resid_one = project(joined, w_skip) + skip_b
    squares = lax.all_gather(after(square_rows, w_kv2, joined), "dp", axis=1, tiled=True)
    w_proj1, w_q2, w_proj2 = squares
    normed = (layer_norm(resid_one, norm1_gain, norm1_bias) + shift).astype(jnp.bfloat16)
    qkv_turned = project_turned(normed, w_qkv) + qkv_b[:, None]
    qkv_heads = qkv_turned.reshape(3 * head_count, head_size, -1)
    self_gains = jnp.stack([qnorm1_gain, knorm1_gain])
    self_biases = jnp.stack([qnorm1_bias, knorm1_bias])
    heads_low = turn_heads(qkv_heads, self_gains, self_biases, tables, head_count)
    kv_own = heads_low[head_count:]
    kv_other = lax.ppermute(kv_own, "dp", pair)
    mixed, self_log = attend(heads_low, [kv_own, kv_other], 2 * kv_own.shape[2])
    fc1_rows = columns(fc1_w)
    w_fc1 = row_gather(after(fc1_rows, squares, mixed))
    grad_in = jnp.concatenate(trade_in(cotangent, is_odd, sizes))
    text_half = jnp.concatenate(ordered(is_odd, *trade_in(text_states, is_odd, sizes)), axis=-1)
    text_other = lax.ppermute(text_half, "dp", pair)
    text_in = jnp.concatenate(ordered(core == 1, text_half, text_other), axis=-1)
    text_count = text_in.shape[0]
    text_in = jnp.pad(text_in, ((0, -text_count % 128), (0, 0)))
    text_in = after(text_in, fc1_rows)
    text_kv = project_back_turned(text_in, w_kv2) + kv2_b[:, None]
    text_low = text_heads(text_kv, knorm2_gain).astype(jnp.bfloat16)
    mixed_low = after(mixed.reshape(model_width, -1).astype(jnp.bfloat16), text_low)
    resid_two = resid_one + project_sublanes(mixed_low, w_proj1) + proj1_b
    w_fc2 = row_gather(after(columns(fc2_w), w_fc1, resid_two))
    cross_in = layer_norm(resid_two, norm3_gain, norm3_bias).astype(jnp.bfloat16)
    cross_heads = project_turned(cross_in, w_q2) + q2_b[:, None]
    cross_heads = cross_heads.reshape(head_count, head_size, -1)
    cross_q = turn_heads(cross_heads, qnorm2_gain[None], qnorm2_bias[None], tables, head_count)
    cross_mixed, cross_log = attend(cross_q, [text_low], text_count)
    cross_low = cross_mixed.reshape(model_width, -1).astype(jnp.bfloat16)
    resid_three = resid_two + project_sublanes(cross_low, w_proj2) + proj2_b
    ffn_in = layer_norm(resid_three, norm2_gain, norm2_bias).astype(jnp.bfloat16)
    pre_act = project(ffn_in, w_fc1) + fc1_b
    hidden = gelu_tanh(pre_act).astype(jnp.bfloat16)
    block_low = (resid_three + project(hidden, w_fc2) + fc2_b).astype(jnp.bfloat16)
    block_out = trade_out(*jnp.split(block_low, 2), is_odd, sizes)

    scatter = partial(column_scatter, place=place, fsdp_size=fsdp_size)
    rows_fc2 = row_scatter(after(low_grad(hidden, grad_in), w_fc2))
    done_fc2 = scatter(rows_fc2)
    bias_fc2 = column_sum(grad_in)
    grad_hidden = project_back(grad_in, w_fc2)
    grad_pre = jax.vjp(gelu_tanh, pre_act)[1](grad_hidden)[0].astype(jnp.bfloat16)
    grad_fc1 = low_grad(ffn_in, grad_pre)
    bias_fc1 = column_sum(grad_pre)
    grad_ffn_in = project_back(grad_pre, w_fc1)
    grad_resid3, gain_n2, bias_n2 = jax.vjp(layer_norm, resid_three, norm2_gain, norm2_bias)[1](
        grad_ffn_in
    )
    grad_resid3 = grad_resid3 + grad_in.astype(jnp.float32)
    grad_branch2 = grad_resid3.astype(jnp.bfloat16)
    grad_proj2 = low_rows(cross_low, grad_branch2)
    bias_proj2 = column_sum(grad_branch2)
    grad_cross = project_back_turned(grad_branch2, w_proj2).reshape(head_count, head_size, -1)
    grad_cq, grad_ckv = attend_back(
        cross_q, grad_cross, cross_mixed, cross_log, [text_low], text_count, [jnp.float32]
    )
    grad_text, gain_kn2 = jax.vjp(text_heads, text_kv, knorm2_gain)[1](
        grad_ckv.reshape(2 * head_count, head_size, -1)
    )
    grad_text = grad_text.astype(jnp.bfloat16)
    grad_kv2 = low_rows(grad_text, text_in)
    bias_kv2 = jnp.sum(grad_text, axis=1, dtype=jnp.float32)
    text_back = project_sublanes(grad_text, w_kv2)[:text_count]
    text_mine, text_theirs = ordered(core == 1, *jnp.split(text_back, 2, axis=-1))
    text_mine = text_mine + lax.ppermute(text_theirs, "dp", pair)
    text_grad = trade_out(*ordered(is_odd, *jnp.split(text_mine, 2, axis=-1)), is_odd, sizes)
    grad_cproj, gain_qn2, bias_qn2 = turn_heads_back(
        cross_heads, grad_cq, [], qnorm2_gain[None], tables, head_count
    )
    gain_qn2, bias_qn2 = gain_qn2[0], bias_qn2[0]
    rows_fc1 = row_scatter(after(grad_fc1, rows_fc2, grad_cproj))
    done_fc1 = scatter(rows_fc1)
    grad_cproj = grad_cproj.reshape(model_width, -1).astype(jnp.bfloat16)
    grad_q2 = low_lanes(cross_in, grad_cproj)
    bias_q2 = jnp.sum(grad_cproj, axis=1, dtype=jnp.float32)
    grad_cross_in = back_sublanes(grad_cproj, w_q2)
    grad_resid2, gain_n3, bias_n3 = jax.vjp(layer_norm, resid_two, norm3_gain, norm3_bias)[1](
        grad_cross_in
    )
    grad_resid2 = grad_resid2 + grad_resid3
    grad_branch1 = grad_resid2.astype(jnp.bfloat16)
    grad_proj1 = low_rows(mixed_low, grad_branch1)
    bias_proj1 = column_sum(grad_branch1)
    grad_mixed = project_back_turned(grad_branch1, w_proj1).reshape(head_count, head_size, -1)
    grad_sq, grad_own, grad_other = attend_back(
        heads_low,
        grad_mixed,
        mixed,
        self_log,
        [kv_own, kv_other],
        2 * kv_own.shape[2],
        [jnp.float32, jnp.bfloat16],
    )
    grad_squares = jnp.stack([grad_proj1, grad_q2, grad_proj2])
    rows_square = lax.psum_scatter(
        after(grad_squares, rows_fc1, grad_sq, done_fc2, block_out), "dp", scatter_dimension=1, tiled=True
    )
    done_square = scatter(rows_square.reshape(-1, model_width))
    done_proj1, done_q2, done_proj2 = jnp.split(done_square, 3)
    kv_shape = kv_own.shape
    grad_taken = lax.ppermute(grad_other, "dp", pair).reshape(kv_shape)
    grad_qkv, self_gain, self_bias = turn_heads_back(
        qkv_heads,
        grad_sq,
        [grad_own.reshape(kv_shape), grad_taken],
        self_gains,
        tables,
        head_count,
    )
    gain_qn1, gain_kn1 = self_gain
    bias_qn1, bias_kn1 = self_bias
    grad_qkv = grad_qkv.reshape(3 * model_width, -1).astype(jnp.bfloat16)
    grad_qkv_w = low_lanes(normed, grad_qkv)
    bias_qkv = jnp.sum(grad_qkv, axis=1, dtype=jnp.float32)
    grad_normed = back_sublanes(grad_qkv, w_qkv)
    grad_shift = jnp.sum(grad_normed, axis=0)
    grad_resid1, gain_n1, bias_n1 = jax.vjp(layer_norm, resid_one, norm1_gain, norm1_bias)[1](
        grad_normed
    )
    grad_resid1 = (grad_resid1 + grad_resid2).astype(jnp.bfloat16)
    rows_qkv = row_scatter(after(grad_qkv_w, rows_square, grad_resid1, done_fc1))
    done_qkv = scatter(rows_qkv)
    grad_skip = low_grad(joined, grad_resid1)
    bias_skip = column_sum(grad_resid1)
    grad_joined = project_back(grad_resid1, w_skip)
    grad_cat, gain_skip, bias_skip_norm = jax.vjp(layer_norm, joined_in, skip_gain, skip_bias)[1](
        grad_joined
    )
    cat_low = grad_cat.astype(jnp.bfloat16)
    both_grad = trade_out(*jnp.split(cat_low, 2), is_odd, sizes)
    vectors = (
        gain_skip,
        bias_skip_norm,
        bias_skip,
        gain_n1,
        bias_n1,
        bias_qkv,
        gain_qn1,
        bias_qn1,
        gain_kn1,
        bias_kn1,
        bias_proj1,
        gain_n3,
        bias_n3,
        bias_q2,
        bias_kv2,
        gain_qn2,
        bias_qn2,
        gain_kn2,
        bias_proj2,
        gain_n2,
        bias_n2,
        bias_fc1,
        bias_fc2,
    )
    sequence = row_place // 2 * 4 + place
    spread_shift = jnp.where(
        jnp.arange(times.shape[0])[:, None] == sequence, grad_shift[None], 0.0
    )
    rows_skip = row_scatter(after(grad_skip, rows_qkv, done_square, cat_low, text_grad))
    done_skip = scatter(rows_skip)
    vector_rows = jnp.concatenate([spread_shift, pack_rows(vectors, model_width)])
    vector_rows = butterfly_sum(vector_rows, "dp", dp_size)
    vector_rows = butterfly_sum(after(vector_rows, both_grad), "fsdp", fsdp_size)
    shift_all = vector_rows[: times.shape[0]]
    summed = unpack_rows(vector_rows[times.shape[0] :], vectors)
    rows_kv2 = row_scatter(after(grad_kv2, rows_skip, done_qkv, vector_rows))
    done_kv2 = scatter(rows_kv2)
    ada_columns = ada_w.shape[1]
    grad_ada = lax.dot_general(
        embed_own.astype(jnp.float32),
        lax.dynamic_slice_in_dim(shift_all, place * ada_columns, ada_columns, 1),
        (((0,), (0,)), ((), ())),
        precision=lax.Precision.HIGHEST,
    )
    bias_ada = jnp.sum(shift_all, axis=0)
    return (
        block_out,
        both_grad[..., :model_width].astype(jnp.float32),
        both_grad[..., model_width:].astype(jnp.float32),
        text_grad,
        summed[0],
        summed[1],
        done_skip,
        summed[2],
        grad_ada,
        bias_ada,
        summed[3],
        summed[4],
        done_qkv,
        summed[5],
        summed[6],
        summed[7],
        summed[8],
        summed[9],
        done_proj1,
        summed[10],
        summed[11],
        summed[12],
        done_q2,
        summed[13],
        done_kv2,
        summed[14],
        summed[15],
        summed[16],
        summed[17],
        done_proj2,
        summed[18],
        summed[19],
        summed[20],
        done_fc1,
        summed[21],
        done_fc2,
        summed[22],
    )


def solution(mesh):
    in_specs = (
        P("dp", "fsdp", None),
        P("dp", "fsdp", None),
        P("dp", None, "fsdp"),
        P("dp"),
        P("dp", None, "fsdp"),
        P("dp", "fsdp", None),
        P(),
        P(),
        P("dp", "fsdp"),
        P(),
        P("dp", "fsdp"),
        P(),
        P(),
        P(),
        P("dp", "fsdp"),
        P(),
        P(),
        P(),
        P(),
        P(),
        P("dp", "fsdp"),
        P(),
        P(),
        P(),
        P("dp", "fsdp"),
        P(),
        P("dp", "fsdp"),
        P(),
        P(),
        P(),
        P(),
        P("dp", "fsdp"),
        P(),
        P(),
        P(),
        P("dp", "fsdp"),
        P(),
        P("dp", "fsdp"),
        P(),
    )
    out_specs = (
        P("dp", "fsdp", None),
        P("dp", "fsdp", None),
        P("dp", "fsdp", None),
        P("dp", None, "fsdp"),
        P(),
        P(),
        P("dp", "fsdp"),
        P(),
        P("dp", "fsdp"),
        P(),
        P(),
        P(),
        P("dp", "fsdp"),
        P(),
        P(),
        P(),
        P(),
        P(),
        P("dp", "fsdp"),
        P(),
        P(),
        P(),
        P("dp", "fsdp"),
        P(),
        P("dp", "fsdp"),
        P(),
        P(),
        P(),
        P(),
        P("dp", "fsdp"),
        P(),
        P(),
        P(),
        P("dp", "fsdp"),
        P(),
        P("dp", "fsdp"),
        P(),
    )
    return jax.shard_map(
        partial(body, mesh.shape["dp"], mesh.shape["fsdp"]),
        mesh=mesh,
        in_specs=in_specs,
        out_specs=out_specs,
        check_vma=False,
    )
```
